512 devices in a mesh: groups: 512 (over x, z, y, core).
Axes of the slice: x: 4, y: 8, z: 8, core: 2. Of those that a mesh axis runs over, the one named last changes fastest.
Arguments:
- currents: bfloat16 [2, 192, 262144], P(None, None, 'groups'), may hold values from -6 to 6
- inverse: bfloat16 [512, 2, 1024, 1024], P('groups'), may hold values from -0.125 to 0.125
- send_blocks: int32 [512, 4], P('groups'), may hold values from 0 to 3
- send_flags: int32 [512, 4], P('groups'), may hold values 0 or 1
Outputs:
- precond: bfloat16 [2, 192, 262144], P(None, None, 'groups')
The draws below stay inside these ranges and needn't reach their ends.
Inputs may be any that keep to these rules, and one draw needn't show every extreme that they name: `send_blocks`: a block index of the lending group's own rows.
All inputs are finite; a program needn't handle non-finite values. No bound on the sum of `send_flags` on one device may be relied on, other than what follows from the above.
Results may differ from the reference program's by a relative error of at most 0.0037.
Values may be sent and summed in bfloat16 or wider, within the bound.
A program may use at most 64 MiB of HBM per device.

```python
import jax
import jax.numpy as jnp
from jax import lax

ORDER = 1024
BLK = 128
COLS = 8
RHS = 192
OWN = 512
GROUPS = 512
ROWS = 262144


def place_ends(drawn, stream_key, smallest, high):
    dims = drawn.shape
    index_at = [jax.random.randint(jax.random.fold_in(stream_key, axis), (), 0, dims[axis]) for axis in range(len(dims))]
    drawn = drawn.at[tuple(index_at)].set(smallest)
    longest = dims.index(max(dims))
    index_at[longest] = (index_at[longest] + 1) % dims[longest]
    return drawn.at[tuple(index_at)].set(high)


def block_levels(own_key, shape, pieces, low, largest):
    def one(axis_at, shards_of):
        steps = jax.random.uniform(jax.random.fold_in(jax.random.fold_in(own_key, 6), axis_at), (shards_of,), jnp.float32, low / len(pieces), largest / len(pieces))
        return jnp.repeat(jnp.exp(steps), shape[axis_at] // shards_of).reshape((-1,) + (1,) * (len(shape) - axis_at - 1))

    loudness = one(*pieces[0])
    for cut in pieces[1:]:
        loudness = loudness * one(*cut)
    return loudness


def noise(stream_key, shape, width, most, shards=(), kind=jnp.bfloat16):
    drawn = width * jax.random.normal(stream_key, shape, jnp.float32)
    if shards:
        drawn = drawn * block_levels(stream_key, shape, shards, -0.22, 0.18)
    return jnp.clip(drawn, -most, most).astype(kind)


def setup_inputs(seed: int = 0) -> dict:
    splits = jax.random.split(jax.random.key(seed), 5)
    return {
        "currents": noise(splits[0], (2, RHS, ROWS), 1.0, 6.0, ((2, 512),)),
        "inverse": noise(splits[1], (GROUPS, 2, ORDER, ORDER), (2 * ORDER) ** -0.5, 0.125, ((0, 512),)),
        "send_blocks": place_ends(jax.random.randint(splits[2], (GROUPS, 4), 0, OWN // BLK), jax.random.fold_in(splits[2], 1), 0, (OWN // BLK) - 1).astype(jnp.int32),
        "send_flags": place_ends((jax.random.randint(splits[3], (GROUPS, 4), 0, 4) < 3).astype(jnp.int32), jax.random.fold_in(splits[3], 1), 0, 1),
    }


def lattice_pairs(groups):
    index = jnp.arange(groups, dtype=jnp.int32)
    column = index % COLS
    lattice_row = index // COLS
    even_column = column % 2 == 0
    even_line = lattice_row % 2 == 0
    first = jnp.where(even_column, index + 1, index - 1)
    second = jnp.where(even_column, index - 1, index + 1)
    third = jnp.where(even_line, index + COLS, index - COLS)
    fourth = jnp.where(even_line, index - COLS, index + COLS)
    partner = jnp.stack([first, second, third, fourth], axis=1)
    partner = (partner + groups) % groups
    return partner.astype(jnp.int32)


def complex_apply(pair):
    matrix, box = pair
    prod = jnp.einsum("prk,qjk->prqj", box.astype(jnp.float32), matrix.astype(jnp.float32))
    return jnp.stack([prod[0, :, 0] - prod[1, :, 1], prod[0, :, 1] + prod[1, :, 0]])


def reference(currents, inverse, send_blocks, send_flags):
    groups = GROUPS
    nblocks = OWN // BLK
    rhs_count = currents.shape[1]
    partner = lattice_pairs(groups)
    active = send_flags.astype(jnp.int32)
    rounds = jnp.arange(4, dtype=jnp.int32)[None, :]
    src_block = send_blocks[partner, rounds]
    src_active = active[partner, rounds]
    blocks = currents.reshape(2, rhs_count, groups, nblocks, BLK)
    slots = blocks[:, :, partner, src_block, :] * src_active[None, None, :, :, None].astype(jnp.bfloat16)
    own_rows = currents.reshape(2, rhs_count, groups, OWN)
    box = jnp.concatenate([own_rows, slots.reshape(2, rhs_count, groups, 4 * BLK)], axis=3)
    box = jnp.transpose(box, (2, 0, 1, 3))
    local = lax.map(complex_apply, (inverse, box))
    total = local[..., :OWN].reshape(groups, 2, rhs_count, nblocks, BLK)
    back = lax.optimization_barrier(local[..., OWN:].astype(jnp.bfloat16)).astype(jnp.float32)
    back = back.reshape(groups, 2, rhs_count, 4, BLK)
    back = jnp.transpose(back, (0, 3, 1, 2, 4)) * src_active[:, :, None, None, None].astype(jnp.float32)
    total = total.at[partner, :, :, src_block, :].add(back)
    total = jnp.transpose(total, (1, 2, 0, 3, 4)).reshape(2, rhs_count, groups * OWN)
    return total.astype(jnp.bfloat16)
```

```python
import functools

import jax
import jax.numpy as jnp
from jax import lax
from jax.experimental import pallas as pl
from jax.experimental.pallas import tpu as pltpu
from jax.sharding import PartitionSpec as P

MESH = pl.DeviceIdType.MESH
BLK = 128
COLS = 8
OWN = 512
ORDER = 1024
RHS = 192
ROUNDS = 4
CHUNKS = 2
RC = RHS // CHUNKS
SEND_ORDER = (3, 2, 1, 0)


def partners(me, count):
    column_odd = lax.rem(me, 2)
    line_odd = lax.rem(me // COLS, 2)
    steps = (
        1 - 2 * column_odd,
        2 * column_odd - 1,
        COLS * (1 - 2 * line_odd),
        COLS * (2 * line_odd - 1),
    )
    return [lax.rem(me + step + count, count) for step in steps]


def kernel(
    count,
    blk_ref,
    flg_ref,
    cur_hbm,
    inv_hbm,
    out_hbm,
    cur,
    mat,
    own,
    slot,
    local,
    lend,
    lent,
    back,
    arrived,
    out,
    load_sem,
    lend_send,
    lend_recv,
    back_send,
    back_recv,
):
    me = lax.axis_index("groups")
    partner = partners(me, count)

    load_cur = pltpu.make_async_copy(cur_hbm, cur, load_sem.at[0])
    load_cur.start()
    barrier = pltpu.get_barrier_semaphore()
    for r in SEND_ORDER:
        pl.semaphore_signal(barrier, inc=1, device_id=(partner[r],), device_id_type=MESH)
    load_mat = []
    for half in range(2):
        for part in range(2):
            load_mat.append(
                pltpu.make_async_copy(
                    inv_hbm.at[0, part, :, pl.ds(half * OWN, OWN)],
                    mat.at[:, pl.ds(half * ORDER + part * OWN, OWN)],
                    load_sem.at[1 + 2 * half + part],
                )
            )
            load_mat[-1].start()

    weight = [
        [
            jnp.where(blk_ref[0, r] == b, flg_ref[0, r], 0).astype(jnp.float32)
            for b in range(OWN // BLK)
        ]
        for r in range(ROUNDS)
    ]
    load_cur.wait()
    for r in range(ROUNDS):
        for c in range(CHUNKS):
            piece = jnp.zeros((2, RC, BLK), jnp.bfloat16)
            for b in range(OWN // BLK):
                block = cur[:, pl.ds(c * RC, RC), pl.ds(b * BLK, BLK)]
                piece += block * weight[r][b].astype(jnp.bfloat16)
            lend[c, r] = piece

    pl.semaphore_wait(barrier, ROUNDS)

    def remote(src, dst, send, recv, c, r):
        return pltpu.make_async_remote_copy(
            src_ref=src.at[c, r],
            dst_ref=dst.at[c, r],
            send_sem=send.at[c, r],
            recv_sem=recv.at[c, r],
            device_id=(partner[r],),
            device_id_type=MESH,
        )

    lends = {}
    for c in range(CHUNKS):
        for r in SEND_ORDER:
            lends[c, r] = remote(lend, lent, lend_send, lend_recv, c, r)
            lends[c, r].start()

    for c in range(CHUNKS):
        real = cur[0, pl.ds(c * RC, RC), :]
        imag = cur[1, pl.ds(c * RC, RC), :]
        own[c, 0, :, pl.ds(0, OWN)] = real
        own[c, 0, :, pl.ds(OWN, OWN)] = -imag
        own[c, 1, :, pl.ds(0, OWN)] = imag
        own[c, 1, :, pl.ds(OWN, OWN)] = real

    def product(rows, matrix):
        return lax.dot_general(
            rows, matrix, (((1,), (1,)), ((), ())), preferred_element_type=jnp.float32
        )

    load_mat[0].wait()
    load_mat[1].wait()
    own_rows = own[...].reshape(2 * RHS, ORDER)
    for half in (1, 0):
        rows = pl.ds(half * OWN, OWN)
        local[:, :, :, rows] = product(own_rows, mat[rows, pl.ds(0, ORDER)]).reshape(
            CHUNKS, 2, RC, OWN
        )
    load_mat[2].wait()
    load_mat[3].wait()

    backs = {}
    for c in range(CHUNKS):
        for r in SEND_ORDER:
            lends[c, r].wait_recv()
            real = lent[c, r, 0]
            imag = lent[c, r, 1]
            slot[c, 0, :, pl.ds(r * BLK, BLK)] = real
            slot[c, 0, :, pl.ds(OWN + r * BLK, BLK)] = -imag
            slot[c, 1, :, pl.ds(r * BLK, BLK)] = imag
            slot[c, 1, :, pl.ds(OWN + r * BLK, BLK)] = real
        slot_rows = slot[c].reshape(2 * RC, ORDER)
        far = pl.ds(OWN, OWN)
        returned = local[c, :, :, far] + product(
            slot_rows, mat[far, pl.ds(ORDER, ORDER)]
        ).reshape(2, RC, OWN)
        for r in SEND_ORDER:
            back[c, r] = returned[:, :, r * BLK : (r + 1) * BLK].astype(jnp.bfloat16)
            backs[c, r] = remote(back, arrived, back_send, back_recv, c, r)
            backs[c, r].start()
        near = pl.ds(0, OWN)
        local[c, :, :, near] += product(slot_rows, mat[near, pl.ds(ORDER, ORDER)]).reshape(
            2, RC, OWN
        )

    stores = []
    for c in range(CHUNKS):
        for r in SEND_ORDER:
            backs[c, r].wait_recv()
        for b in range(OWN // BLK):
            total = local[c, :, :, pl.ds(b * BLK, BLK)]
            for r in range(ROUNDS):
                total += arrived[c, r].astype(jnp.float32) * weight[r][b]
            out[:, pl.ds(c * RC, RC), pl.ds(b * BLK, BLK)] = total.astype(jnp.bfloat16)
        stores.append(
            pltpu.make_async_copy(
                out.at[:, pl.ds(c * RC, RC), :],
                out_hbm.at[:, pl.ds(c * RC, RC), :],
                load_sem.at[5 + c],
            )
        )
        stores[-1].start()
    for copy in stores:
        copy.wait()
    for c in range(CHUNKS):
        for r in range(ROUNDS):
            lends[c, r].wait_send()
            backs[c, r].wait_send()


def solution(mesh):
    count = mesh.shape["groups"]

    def step(currents, inverse, send_blocks, send_flags):
        pieces = (CHUNKS, ROUNDS, 2, RC, BLK)
        return pl.pallas_call(
            functools.partial(kernel, count),
            out_shape=jax.ShapeDtypeStruct(currents.shape, jnp.bfloat16),
            in_specs=[
                pl.BlockSpec(memory_space=pltpu.SMEM),
                pl.BlockSpec(memory_space=pltpu.SMEM),
                pl.BlockSpec(memory_space=pl.ANY),
                pl.BlockSpec(memory_space=pl.ANY),
            ],
            out_specs=pl.BlockSpec(memory_space=pl.ANY),
            scratch_shapes=[
                pltpu.VMEM((2, RHS, OWN), jnp.bfloat16),
                pltpu.VMEM((ORDER, 2 * ORDER), jnp.bfloat16),
                pltpu.VMEM((CHUNKS, 2, RC, ORDER), jnp.bfloat16),
                pltpu.VMEM((CHUNKS, 2, RC, ORDER), jnp.bfloat16),
                pltpu.VMEM((CHUNKS, 2, RC, ORDER), jnp.float32),
                pltpu.VMEM(pieces, jnp.bfloat16),
                pltpu.VMEM(pieces, jnp.bfloat16),
                pltpu.VMEM(pieces, jnp.bfloat16),
                pltpu.VMEM(pieces, jnp.bfloat16),
                pltpu.VMEM((2, RHS, OWN), jnp.bfloat16),
                pltpu.SemaphoreType.DMA((5 + CHUNKS,)),
                pltpu.SemaphoreType.DMA((CHUNKS, ROUNDS)),
                pltpu.SemaphoreType.DMA((CHUNKS, ROUNDS)),
                pltpu.SemaphoreType.DMA((CHUNKS, ROUNDS)),
                pltpu.SemaphoreType.DMA((CHUNKS, ROUNDS)),
            ],
            compiler_params=pltpu.CompilerParams(
                collective_id=1,
                has_side_effects=True,
                vmem_limit_bytes=60 * 1024 * 1024,
            ),
            cost_estimate=pl.CostEstimate(
                flops=8 * RHS * ORDER * ORDER,
                bytes_accessed=4 * ORDER * ORDER + 8 * RHS * OWN,
                transcendentals=0,
            ),
        )(send_blocks, send_flags, currents, inverse)

    in_specs = (
        P(None, None, "groups"),
        P("groups", None, None, None),
        P("groups", None),
        P("groups", None),
    )
    return jax.shard_map(
        step, mesh=mesh, in_specs=in_specs, out_specs=P(None, None, "groups"), check_vma=False
    )
```

```python
import functools

import jax
import jax.numpy as jnp
from jax import lax
from jax.experimental import pallas as pl
from jax.experimental.pallas import tpu as pltpu
from jax.sharding import PartitionSpec as P

MESH = pl.DeviceIdType.MESH
BLK = 128
COLS = 8
OWN = 512
ORDER = 1024
RHS = 192
ROUNDS = 4
PLANE = 128
CHUNKS = 2
RC = RHS // CHUNKS
SEND_ORDER = (3, 2, 1, 0)


def partners(me, count):
    column_odd = lax.rem(me, 2)
    line_odd = lax.rem(me // COLS, 2)
    steps = (
        1 - 2 * column_odd,
        2 * column_odd - 1,
        COLS * (1 - 2 * line_odd),
        COLS * (2 * line_odd - 1),
    )
    return [lax.rem(me + step + count, count) for step in steps]


def ends(me):
    line = lax.rem(me // COLS, PLANE // COLS)
    column = lax.rem(me, PLANE)
    first = (None, column == 0, None, line == 0)
    last = (None, column == PLANE - 1, None, line == PLANE // COLS - 1)
    return first, last


def kernel(
    count,
    blk_ref,
    flg_ref,
    cur_hbm,
    inv_hbm,
    out,
    cur,
    mat,
    own,
    slot,
    local,
    lend,
    lent,
    back,
    arrived,
    load_sem,
    lend_send,
    lend_recv,
    back_send,
    back_recv,
    ready,
):
    me = lax.axis_index("groups")
    partner = partners(me, count)

    load_cur = pltpu.make_async_copy(cur_hbm, cur, load_sem.at[0])
    load_cur.start()
    barrier = pltpu.get_barrier_semaphore()
    first, last = ends(me)

    def greet(r):
        pl.semaphore_signal(barrier, inc=1, device_id=(partner[r],), device_id_type=MESH)

    def unless(condition, do):
        if condition is None:
            do()
        else:
            pl.when(jnp.logical_not(condition))(do)

    for r in SEND_ORDER:
        unless(last[r], functools.partial(greet, r))
    load_mat = []
    for half in range(2):
        for part in range(2):
            load_mat.append(
                pltpu.make_async_copy(
                    inv_hbm.at[0, part, :, pl.ds(half * OWN, OWN)],
                    mat.at[:, pl.ds(half * ORDER + part * OWN, OWN)],
                    load_sem.at[1 + 2 * half + part],
                )
            )
            load_mat[-1].start()

    weight = [
        [
            jnp.where(blk_ref[0, r] == b, flg_ref[0, r], 0).astype(jnp.float32)
            for b in range(OWN // BLK)
        ]
        for r in range(ROUNDS)
    ]
    load_cur.wait()
    for r in range(ROUNDS):
        for c in range(CHUNKS):
            piece = jnp.zeros((2, RC, BLK), jnp.bfloat16)
            for b in range(OWN // BLK):
                block = cur[:, pl.ds(c * RC, RC), pl.ds(b * BLK, BLK)]
                piece += block * weight[r][b].astype(jnp.bfloat16)
            lend[c, r] = piece

    greeted = ROUNDS
    for r in (1, 3):
        greeted = greeted - first[r].astype(jnp.int32)
    pl.semaphore_wait(barrier, greeted)
    for r in (3, 1):

        @pl.when(last[r])
        def _():
            pl.semaphore_signal(
                ready.at[r], inc=1, device_id=(partner[r],), device_id_type=MESH
            )

    def remote(src, dst, send, recv, c, r):
        return pltpu.make_async_remote_copy(
            src_ref=src.at[c, r],
            dst_ref=dst.at[c, r],
            send_sem=send.at[c, r],
            recv_sem=recv.at[c, r],
            device_id=(partner[r],),
            device_id_type=MESH,
        )

    lends = {}
    for c in range(CHUNKS):
        for r in SEND_ORDER:
            lends[c, r] = remote(lend, lent, lend_send, lend_recv, c, r)
            unless(first[r], lends[c, r].start)

    for c in range(CHUNKS):
        real = cur[0, pl.ds(c * RC, RC), :]
        imag = cur[1, pl.ds(c * RC, RC), :]
        own[c, 0, :, pl.ds(0, OWN)] = real
        own[c, 0, :, pl.ds(OWN, OWN)] = -imag
        own[c, 1, :, pl.ds(0, OWN)] = imag
        own[c, 1, :, pl.ds(OWN, OWN)] = real

    def product(rows, matrix):
        return lax.dot_general(
            rows, matrix, (((1,), (1,)), ((), ())), preferred_element_type=jnp.float32
        )

    load_mat[0].wait()
    load_mat[1].wait()
    own_rows = own[...].reshape(2 * RHS, ORDER)
    for half in (1, 0):
        rows = pl.ds(half * OWN, OWN)
        local[:, :, :, rows] = product(own_rows, mat[rows, pl.ds(0, ORDER)]).reshape(
            CHUNKS, 2, RC, OWN
        )
    load_mat[2].wait()
    load_mat[3].wait()
    for r in (3, 1):

        @pl.when(first[r])
        def _():
            pl.semaphore_wait(ready.at[r], 1)
            for c in range(CHUNKS):
                lends[c, r].start()

    backs = {}
    for c in range(CHUNKS):
        for r in SEND_ORDER:
            lends[c, r].wait_recv()
            real = lent[c, r, 0]
            imag = lent[c, r, 1]
            slot[c, 0, :, pl.ds(r * BLK, BLK)] = real
            slot[c, 0, :, pl.ds(OWN + r * BLK, BLK)] = -imag
            slot[c, 1, :, pl.ds(r * BLK, BLK)] = imag
            slot[c, 1, :, pl.ds(OWN + r * BLK, BLK)] = real
        slot_rows = slot[c].reshape(2 * RC, ORDER)
        far = pl.ds(OWN, OWN)
        returned = local[c, :, :, far] + product(
            slot_rows, mat[far, pl.ds(ORDER, ORDER)]
        ).reshape(2, RC, OWN)
        for r in SEND_ORDER:
            back[c, r] = returned[:, :, r * BLK : (r + 1) * BLK].astype(jnp.bfloat16)
            backs[c, r] = remote(back, arrived, back_send, back_recv, c, r)
            if r == 3:
                backs[c, r].start()
            else:
                unless(last[3], backs[c, r].start)
        near = pl.ds(0, OWN)
        local[c, :, :, near] += product(slot_rows, mat[near, pl.ds(ORDER, ORDER)]).reshape(
            2, RC, OWN
        )

    @pl.when(last[3])
    def _():
        for c in range(CHUNKS):
            backs[c, 3].wait_send()
        for r in (2, 1, 0):
            for c in range(CHUNKS):
                backs[c, r].start()

    for c in range(CHUNKS):
        for r in SEND_ORDER:
            backs[c, r].wait_recv()
        for b in range(OWN // BLK):
            total = local[c, :, :, pl.ds(b * BLK, BLK)]
            for r in range(ROUNDS):
                total += arrived[c, r].astype(jnp.float32) * weight[r][b]
            out[:, pl.ds(c * RC, RC), pl.ds(b * BLK, BLK)] = total.astype(jnp.bfloat16)
    for c in range(CHUNKS):
        for r in range(ROUNDS):
            lends[c, r].wait_send()
            if r == 3:
                unless(last[3], backs[c, r].wait_send)
            else:
                backs[c, r].wait_send()


def solution(mesh):
    count = mesh.shape["groups"]

    def step(currents, inverse, send_blocks, send_flags):
        pieces = (CHUNKS, ROUNDS, 2, RC, BLK)
        return pl.pallas_call(
            functools.partial(kernel, count),
            out_shape=pltpu.VMEM(currents.shape, jnp.bfloat16),
            in_specs=[
                pl.BlockSpec(memory_space=pltpu.SMEM),
                pl.BlockSpec(memory_space=pltpu.SMEM),
                pl.BlockSpec(memory_space=pl.ANY),
                pl.BlockSpec(memory_space=pl.ANY),
            ],
            out_specs=pl.BlockSpec(memory_space=pltpu.VMEM),
            scratch_shapes=[
                pltpu.VMEM((2, RHS, OWN), jnp.bfloat16),
                pltpu.VMEM((ORDER, 2 * ORDER), jnp.bfloat16),
                pltpu.VMEM((CHUNKS, 2, RC, ORDER), jnp.bfloat16),
                pltpu.VMEM((CHUNKS, 2, RC, ORDER), jnp.bfloat16),
                pltpu.VMEM((CHUNKS, 2, RC, ORDER), jnp.float32),
                pltpu.VMEM(pieces, jnp.bfloat16),
                pltpu.VMEM(pieces, jnp.bfloat16),
                pltpu.VMEM(pieces, jnp.bfloat16),
                pltpu.VMEM(pieces, jnp.bfloat16),
                pltpu.SemaphoreType.DMA((5,)),
                pltpu.SemaphoreType.DMA((CHUNKS, ROUNDS)),
                pltpu.SemaphoreType.DMA((CHUNKS, ROUNDS)),
                pltpu.SemaphoreType.DMA((CHUNKS, ROUNDS)),
                pltpu.SemaphoreType.DMA((CHUNKS, ROUNDS)),
                pltpu.SemaphoreType.REGULAR((ROUNDS,)),
            ],
            compiler_params=pltpu.CompilerParams(
                collective_id=1,
                has_side_effects=True,
                vmem_limit_bytes=60 * 1024 * 1024,
            ),
            cost_estimate=pl.CostEstimate(
                flops=8 * RHS * ORDER * ORDER,
                bytes_accessed=4 * ORDER * ORDER + 8 * RHS * OWN,
                transcendentals=0,
            ),
        )(send_blocks, send_flags, currents, inverse)

    in_specs = (
        P(None, None, "groups"),
        P("groups", None, None, None),
        P("groups", None),
        P("groups", None),
    )
    return jax.shard_map(
        step, mesh=mesh, in_specs=in_specs, out_specs=P(None, None, "groups"), check_vma=False
    )
```

```python
import functools

import jax
import jax.numpy as jnp
from jax import lax
from jax.experimental import pallas as pl
from jax.experimental.pallas import tpu as pltpu
from jax.sharding import PartitionSpec as P

MESH = pl.DeviceIdType.MESH
BLK = 128
COLS = 8
OWN = 512
ORDER = 1024
RHS = 192
ROUNDS = 4
PLANE = 128
CHUNKS = 2
RC = RHS // CHUNKS
SEND_ORDER = (3, 2, 1, 0)


def partners(me, count):
    column_odd = lax.rem(me, 2)
    line_odd = lax.rem(me // COLS, 2)
    steps = (
        1 - 2 * column_odd,
        2 * column_odd - 1,
        COLS * (1 - 2 * line_odd),
        COLS * (2 * line_odd - 1),
    )
    return [lax.rem(me + step + count, count) for step in steps]


def ends(me):
    line = lax.rem(me // COLS, PLANE // COLS)
    column = lax.rem(me, PLANE)
    first = (None, column == 0, None, line == 0)
    last = (None, column == PLANE - 1, None, line == PLANE // COLS - 1)
    return first, last


def kernel(
    count,
    blk_ref,
    flg_ref,
    cur_hbm,
    inv_hbm,
    out,
    cur,
    mat,
    own,
    slot,
    local,
    lend,
    lent,
    back,
    arrived,
    load_sem,
    lend_send,
    lend_recv,
    back_send,
    back_recv,
    ready,
    edge,
    wedge,
    wedge_send,
    wedge_recv,
):
    me = lax.axis_index("groups")
    partner = partners(me, count)

    load_cur = pltpu.make_async_copy(cur_hbm, cur, load_sem.at[0])
    load_cur.start()
    barrier = pltpu.get_barrier_semaphore()
    first, last = ends(me)

    def greet(r):
        pl.semaphore_signal(barrier, inc=1, device_id=(partner[r],), device_id_type=MESH)

    def unless(condition, do):
        if condition is None:
            do()
        else:
            pl.when(jnp.logical_not(condition))(do)

    for r in SEND_ORDER:
        unless(last[r], functools.partial(greet, r))
    load_mat = []
    for half in range(2):
        for part in range(2):
            load_mat.append(
                pltpu.make_async_copy(
                    inv_hbm.at[0, part, :, pl.ds(half * OWN, OWN)],
                    mat.at[:, pl.ds(half * ORDER + part * OWN, OWN)],
                    load_sem.at[1 + 2 * half + part],
                )
            )
            load_mat[-1].start()

    weight = [
        [
            jnp.where(blk_ref[0, r] == b, flg_ref[0, r], 0).astype(jnp.float32)
            for b in range(OWN // BLK)
        ]
        for r in range(ROUNDS)
    ]
    load_cur.wait()
    for r in range(ROUNDS):
        for c in range(CHUNKS):
            piece = jnp.zeros((2, RC, BLK), jnp.bfloat16)
            for b in range(OWN // BLK):
                block = cur[:, pl.ds(c * RC, RC), pl.ds(b * BLK, BLK)]
                piece += block * weight[r][b].astype(jnp.bfloat16)
            lend[c, r] = piece

    greeted = ROUNDS
    for r in (1, 3):
        greeted = greeted - first[r].astype(jnp.int32)
    pl.semaphore_wait(barrier, greeted)
    for r in (3, 1):

        @pl.when(last[r])
        def _():
            pl.semaphore_signal(
                ready.at[r], inc=1, device_id=(partner[r],), device_id_type=MESH
            )

    def remote(src, dst, send, recv, c, r):
        return pltpu.make_async_remote_copy(
            src_ref=src.at[c, r],
            dst_ref=dst.at[c, r],
            send_sem=send.at[c, r],
            recv_sem=recv.at[c, r],
            device_id=(partner[r],),
            device_id_type=MESH,
        )

    gives = last[3] & (lax.rem(me, PLANE) != PLANE - COLS)
    takes = first[3] & (lax.rem(me, PLANE) != 0)
    lends = {}
    for c in range(CHUNKS):
        for r in range(ROUNDS):
            lends[c, r] = remote(lend, lent, lend_send, lend_recv, c, r)
    plane_end = lax.rem(me // COLS, PLANE // COLS) == PLANE // COLS - 2
    for c in range(CHUNKS):
        for r in SEND_ORDER:
            if r == 3:
                pl.when(jnp.logical_not(first[3] | plane_end))(lends[c, r].start)
            else:
                unless(first[r], lends[c, r].start)
    for c in range(CHUNKS):
        pl.when(plane_end)(lends[c, 3].start)

    for c in range(CHUNKS):
        real = cur[0, pl.ds(c * RC, RC), :]
        imag = cur[1, pl.ds(c * RC, RC), :]
        own[c, 0, :, pl.ds(0, OWN)] = real
        own[c, 0, :, pl.ds(OWN, OWN)] = -imag
        own[c, 1, :, pl.ds(0, OWN)] = imag
        own[c, 1, :, pl.ds(OWN, OWN)] = real

    def product(rows, matrix):
        return lax.dot_general(
            rows, matrix, (((1,), (1,)), ((), ())), preferred_element_type=jnp.float32
        )

    load_mat[0].wait()
    load_mat[1].wait()
    own_rows = own[...].reshape(2 * RHS, ORDER)
    for half in (1, 0):
        rows = pl.ds(half * OWN, OWN)
        local[:, :, :, rows] = product(own_rows, mat[rows, pl.ds(0, ORDER)]).reshape(
            CHUNKS, 2, RC, OWN
        )
    load_mat[2].wait()
    load_mat[3].wait()
    for r in (1, 3):

        @pl.when(first[r])
        def _():
            pl.semaphore_wait(ready.at[r], 1)
            for c in range(CHUNKS):
                lends[c, r].start()

    corner = pltpu.make_async_remote_copy(
        src_ref=edge,
        dst_ref=wedge,
        send_sem=wedge_send,
        recv_sem=wedge_recv,
        device_id=(partner[3],),
        device_id_type=MESH,
    )

    def fill(c, r):
        lends[c, r].wait_recv()
        real = lent[c, r, 0]
        imag = lent[c, r, 1]
        slot[c, 0, :, pl.ds(r * BLK, BLK)] = real
        slot[c, 0, :, pl.ds(OWN + r * BLK, BLK)] = -imag
        slot[c, 1, :, pl.ds(r * BLK, BLK)] = imag
        slot[c, 1, :, pl.ds(OWN + r * BLK, BLK)] = real

    backs = {}
    for c in range(CHUNKS):
        for r in range(ROUNDS):
            backs[c, r] = remote(back, arrived, back_send, back_recv, c, r)

    @pl.when(gives)
    def _():
        tail = pl.ds(ORDER - BLK, BLK)
        for part in range(2):
            edge[:, pl.ds(part * BLK, BLK)] = mat[tail, pl.ds(ORDER + (1 + part) * OWN - BLK, BLK)]
        corner.start()
        for c in range(CHUNKS):
            for r in (0, 1, 2):
                fill(c, r)
            part = local[c, :, :, tail].reshape(2 * RC, BLK)
            for half in range(2):
                part += product(
                    slot[c, :, :, pl.ds(half * OWN, OWN - BLK)].reshape(2 * RC, OWN - BLK),
                    mat[tail, pl.ds(ORDER + half * OWN, OWN - BLK)],
                )
            back[c, 3] = part.reshape(2, RC, BLK).astype(jnp.bfloat16)
            backs[c, 3].start()

    for c in range(CHUNKS):

        @pl.when(jnp.logical_not(gives))
        def _():
            for r in (0, 1, 2):
                fill(c, r)

        fill(c, 3)
        slot_rows = slot[c].reshape(2 * RC, ORDER)
        far = pl.ds(OWN, OWN)
        returned = local[c, :, :, far] + product(
            slot_rows, mat[far, pl.ds(ORDER, ORDER)]
        ).reshape(2, RC, OWN)
        for r in SEND_ORDER:
            piece = returned[:, :, r * BLK : (r + 1) * BLK].astype(jnp.bfloat16)
            if r == 3:

                @pl.when(jnp.logical_not(gives))
                def _():
                    back[c, r] = piece
                    backs[c, r].start()

            else:
                back[c, r] = piece
                if r == 1:
                    pl.when(last[1] | jnp.logical_not(last[3]))(backs[c, r].start)
                else:
                    unless(last[3], backs[c, r].start)
        near = pl.ds(0, OWN)
        local[c, :, :, near] += product(slot_rows, mat[near, pl.ds(ORDER, ORDER)]).reshape(
            2, RC, OWN
        )

    @pl.when(last[3])
    def _():
        for c in range(CHUNKS):
            backs[c, 3].wait_send()
        for r in (2, 1, 0):
            for c in range(CHUNKS):
                unless(last[1] if r == 1 else None, backs[c, r].start)

    @pl.when(takes)
    def _():
        corner.wait_recv()
        for c in range(CHUNKS):
            real = lend[c, 3, 0]
            imag = lend[c, 3, 1]
            mine = jnp.concatenate(
                [
                    jnp.concatenate([real, -imag], axis=1),
                    jnp.concatenate([imag, real], axis=1),
                ],
                axis=0,
            )
            extra = product(mine, wedge[...]).reshape(2, RC, BLK)
            for b in range(OWN // BLK):
                local[c, :, :, pl.ds(b * BLK, BLK)] += extra * weight[3][b]

    for c in range(CHUNKS):
        for r in SEND_ORDER:
            backs[c, r].wait_recv()
        for b in range(OWN // BLK):
            total = local[c, :, :, pl.ds(b * BLK, BLK)]
            for r in range(ROUNDS):
                total += arrived[c, r].astype(jnp.float32) * weight[r][b]
            out[:, pl.ds(c * RC, RC), pl.ds(b * BLK, BLK)] = total.astype(jnp.bfloat16)
    @pl.when(gives)
    def _():
        corner.wait_send()

    for c in range(CHUNKS):
        for r in range(ROUNDS):
            lends[c, r].wait_send()
            if r == 3:
                unless(last[3], backs[c, r].wait_send)
            else:
                backs[c, r].wait_send()


def solution(mesh):
    count = mesh.shape["groups"]

    def step(currents, inverse, send_blocks, send_flags):
        pieces = (CHUNKS, ROUNDS, 2, RC, BLK)
        return pl.pallas_call(
            functools.partial(kernel, count),
            out_shape=pltpu.VMEM(currents.shape, jnp.bfloat16),
            in_specs=[
                pl.BlockSpec(memory_space=pltpu.SMEM),
                pl.BlockSpec(memory_space=pltpu.SMEM),
                pl.BlockSpec(memory_space=pl.ANY),
                pl.BlockSpec(memory_space=pl.ANY),
            ],
            out_specs=pl.BlockSpec(memory_space=pltpu.VMEM),
            scratch_shapes=[
                pltpu.VMEM((2, RHS, OWN), jnp.bfloat16),
                pltpu.VMEM((ORDER, 2 * ORDER), jnp.bfloat16),
                pltpu.VMEM((CHUNKS, 2, RC, ORDER), jnp.bfloat16),
                pltpu.VMEM((CHUNKS, 2, RC, ORDER), jnp.bfloat16),
                pltpu.VMEM((CHUNKS, 2, RC, ORDER), jnp.float32),
                pltpu.VMEM(pieces, jnp.bfloat16),
                pltpu.VMEM(pieces, jnp.bfloat16),
                pltpu.VMEM(pieces, jnp.bfloat16),
                pltpu.VMEM(pieces, jnp.bfloat16),
                pltpu.SemaphoreType.DMA((5,)),
                pltpu.SemaphoreType.DMA((CHUNKS, ROUNDS)),
                pltpu.SemaphoreType.DMA((CHUNKS, ROUNDS)),
                pltpu.SemaphoreType.DMA((CHUNKS, ROUNDS)),
                pltpu.SemaphoreType.DMA((CHUNKS, ROUNDS)),
                pltpu.SemaphoreType.REGULAR((ROUNDS,)),
                pltpu.VMEM((BLK, 2 * BLK), jnp.bfloat16),
                pltpu.VMEM((BLK, 2 * BLK), jnp.bfloat16),
                pltpu.SemaphoreType.DMA,
                pltpu.SemaphoreType.DMA,
            ],
            compiler_params=pltpu.CompilerParams(
                collective_id=1,
                has_side_effects=True,
                vmem_limit_bytes=60 * 1024 * 1024,
            ),
            cost_estimate=pl.CostEstimate(
                flops=8 * RHS * ORDER * ORDER,
                bytes_accessed=4 * ORDER * ORDER + 8 * RHS * OWN,
                transcendentals=0,
            ),
        )(send_blocks, send_flags, currents, inverse)

    in_specs = (
        P(None, None, "groups"),
        P("groups", None, None, None),
        P("groups", None),
        P("groups", None),
    )
    return jax.shard_map(
        step, mesh=mesh, in_specs=in_specs, out_specs=P(None, None, "groups"), check_vma=False
    )
```

```python
import functools

import jax
import jax.numpy as jnp
from jax import lax
from jax.experimental import pallas as pl
from jax.experimental.pallas import tpu as pltpu
from jax.sharding import PartitionSpec as P

MESH = pl.DeviceIdType.MESH
BLK = 128
COLS = 8
OWN = 512
ORDER = 1024
RHS = 192
ROUNDS = 4
PLANE = 128
CHUNKS = 2
RC = RHS // CHUNKS
SEND_ORDER = (3, 2, 1, 0)


def partners(me, count):
    column_odd = lax.rem(me, 2)
    line_odd = lax.rem(me // COLS, 2)
    steps = (
        1 - 2 * column_odd,
        2 * column_odd - 1,
        COLS * (1 - 2 * line_odd),
        COLS * (2 * line_odd - 1),
    )
    return [lax.rem(me + step + count, count) for step in steps]


def ends(me):
    line = lax.rem(me // COLS, PLANE // COLS)
    column = lax.rem(me, PLANE)
    first = (None, column == 0, None, line == 0)
    last = (None, column == PLANE - 1, None, line == PLANE // COLS - 1)
    return first, last, line == 1


def kernel(
    count,
    blk_ref,
    flg_ref,
    cur_hbm,
    inv_hbm,
    out,
    cur,
    mat,
    own,
    slot,
    local,
    lend,
    lent,
    back,
    arrived,
    load_sem,
    lend_send,
    lend_recv,
    back_send,
    back_recv,
    ready,
    relay,
    relay_send,
    relay_recv,
    edge,
    wedge,
    wedge_send,
    wedge_recv,
):
    me = lax.axis_index("groups")
    partner = partners(me, count)

    load_cur = pltpu.make_async_copy(cur_hbm, cur, load_sem.at[0])
    load_cur.start()
    barrier = pltpu.get_barrier_semaphore()
    first, last, hub = ends(me)
    before = lax.rem(me + count - 2 * COLS, count)
    after = lax.rem(me + 2 * COLS, count)

    def greet(r):
        pl.semaphore_signal(barrier, inc=1, device_id=(partner[r],), device_id_type=MESH)

    def unless(condition, do):
        if condition is None:
            do()
        else:
            pl.when(jnp.logical_not(condition))(do)

    for r in SEND_ORDER:
        unless(last[r], functools.partial(greet, r))

    @pl.when(hub)
    def _():
        pl.semaphore_signal(barrier, inc=1, device_id=(before,), device_id_type=MESH)

    load_mat = []
    for half in range(2):
        for part in range(2):
            load_mat.append(
                pltpu.make_async_copy(
                    inv_hbm.at[0, part, :, pl.ds(half * OWN, OWN)],
                    mat.at[:, pl.ds(half * ORDER + part * OWN, OWN)],
                    load_sem.at[1 + 2 * half + part],
                )
            )
            load_mat[-1].start()

    weight = [
        [
            jnp.where(blk_ref[0, r] == b, flg_ref[0, r], 0).astype(jnp.float32)
            for b in range(OWN // BLK)
        ]
        for r in range(ROUNDS)
    ]
    load_cur.wait()
    for r in range(ROUNDS):
        for c in range(CHUNKS):
            piece = jnp.zeros((2, RC, BLK), jnp.bfloat16)
            for b in range(OWN // BLK):
                block = cur[:, pl.ds(c * RC, RC), pl.ds(b * BLK, BLK)]
                piece += block * weight[r][b].astype(jnp.bfloat16)
            lend[c, r] = piece

    greeted = ROUNDS
    for r in (1, 3):
        greeted = greeted - first[r].astype(jnp.int32)
    pl.semaphore_wait(barrier, greeted + last[3].astype(jnp.int32))
    for r in (3, 1):

        @pl.when(last[r])
        def _():
            pl.semaphore_signal(
                ready.at[r], inc=1, device_id=(partner[r],), device_id_type=MESH
            )

    def remote(src, dst, send, recv, c, r):
        return pltpu.make_async_remote_copy(
            src_ref=src.at[c, r],
            dst_ref=dst.at[c, r],
            send_sem=send.at[c, r],
            recv_sem=recv.at[c, r],
            device_id=(partner[r],),
            device_id_type=MESH,
        )

    gives = last[3]
    takes = first[3]
    lends = {}
    for c in range(CHUNKS):
        for r in range(ROUNDS):
            lends[c, r] = remote(lend, lent, lend_send, lend_recv, c, r)
    legs = []
    for c in range(CHUNKS):
        legs.append(
            (
                pltpu.make_async_remote_copy(
                    src_ref=lend.at[c, 3],
                    dst_ref=relay.at[c],
                    send_sem=lend_send.at[c, 3],
                    recv_sem=relay_recv.at[c],
                    device_id=(after,),
                    device_id_type=MESH,
                ),
                pltpu.make_async_remote_copy(
                    src_ref=relay.at[c],
                    dst_ref=lent.at[c, 3],
                    send_sem=relay_send.at[c],
                    recv_sem=lend_recv.at[c, 3],
                    device_id=(partner[2],),
                    device_id_type=MESH,
                ),
            )
        )
    for c in range(CHUNKS):
        pl.when(last[3])(legs[c][0].start)
    plane_end = lax.rem(me // COLS, PLANE // COLS) == PLANE // COLS - 2
    for c in range(CHUNKS):
        for r in SEND_ORDER:
            if r == 3:
                pl.when(jnp.logical_not(first[3] | last[3] | plane_end))(lends[c, r].start)
            else:
                unless(first[r], lends[c, r].start)
    for c in range(CHUNKS):
        pl.when(plane_end)(lends[c, 3].start)

    for c in range(CHUNKS):
        real = cur[0, pl.ds(c * RC, RC), :]
        imag = cur[1, pl.ds(c * RC, RC), :]
        own[c, 0, :, pl.ds(0, OWN)] = real
        own[c, 0, :, pl.ds(OWN, OWN)] = -imag
        own[c, 1, :, pl.ds(0, OWN)] = imag
        own[c, 1, :, pl.ds(OWN, OWN)] = real

    def product(rows, matrix):
        return lax.dot_general(
            rows, matrix, (((1,), (1,)), ((), ())), preferred_element_type=jnp.float32
        )

    load_mat[0].wait()
    load_mat[1].wait()
    own_rows = own[...].reshape(2 * RHS, ORDER)
    for half in (1, 0):
        rows = pl.ds(half * OWN, OWN)
        local[:, :, :, rows] = product(own_rows, mat[rows, pl.ds(0, ORDER)]).reshape(
            CHUNKS, 2, RC, OWN
        )
    load_mat[2].wait()
    load_mat[3].wait()
    @pl.when(hub)
    def _():
        for c in range(CHUNKS):
            legs[c][0].wait_recv()
            legs[c][1].start()

    for r in (1, 3):

        @pl.when(first[r])
        def _():
            pl.semaphore_wait(ready.at[r], 1)
            for c in range(CHUNKS):
                lends[c, r].start()

    corner = pltpu.make_async_remote_copy(
        src_ref=edge,
        dst_ref=wedge,
        send_sem=wedge_send,
        recv_sem=wedge_recv,
        device_id=(partner[3],),
        device_id_type=MESH,
    )

    def fill(c, r):
        lends[c, r].wait_recv()
        real = lent[c, r, 0]
        imag = lent[c, r, 1]
        slot[c, 0, :, pl.ds(r * BLK, BLK)] = real
        slot[c, 0, :, pl.ds(OWN + r * BLK, BLK)] = -imag
        slot[c, 1, :, pl.ds(r * BLK, BLK)] = imag
        slot[c, 1, :, pl.ds(OWN + r * BLK, BLK)] = real

    backs = {}
    for c in range(CHUNKS):
        for r in range(ROUNDS):
            backs[c, r] = remote(back, arrived, back_send, back_recv, c, r)

    @pl.when(gives)
    def _():
        tail = pl.ds(ORDER - BLK, BLK)
        for part in range(2):
            edge[:, pl.ds(part * BLK, BLK)] = mat[tail, pl.ds(ORDER + (1 + part) * OWN - BLK, BLK)]
        corner.start()
        for c in range(CHUNKS):
            for r in (0, 1, 2):
                fill(c, r)
            part = local[c, :, :, tail].reshape(2 * RC, BLK)
            for half in range(2):
                part += product(
                    slot[c, :, :, pl.ds(half * OWN, OWN - BLK)].reshape(2 * RC, OWN - BLK),
                    mat[tail, pl.ds(ORDER + half * OWN, OWN - BLK)],
                )
            back[c, 3] = part.reshape(2, RC, BLK).astype(jnp.bfloat16)
            backs[c, 3].start()

    for c in range(CHUNKS):

        @pl.when(jnp.logical_not(gives))
        def _():
            for r in (0, 1, 2):
                fill(c, r)

        fill(c, 3)
        slot_rows = slot[c].reshape(2 * RC, ORDER)
        far = pl.ds(OWN, OWN)
        returned = local[c, :, :, far] + product(
            slot_rows, mat[far, pl.ds(ORDER, ORDER)]
        ).reshape(2, RC, OWN)
        for r in (2, 1, 0, 3):
            piece = returned[:, :, r * BLK : (r + 1) * BLK].astype(jnp.bfloat16)
            if r == 3:

                @pl.when(jnp.logical_not(gives))
                def _():
                    back[c, r] = piece
                    backs[c, r].start()

            else:
                back[c, r] = piece
                if r == 1:
                    pl.when(last[1] | jnp.logical_not(last[3]))(backs[c, r].start)
                else:
                    unless(last[3], backs[c, r].start)
        near = pl.ds(0, OWN)
        local[c, :, :, near] += product(slot_rows, mat[near, pl.ds(ORDER, ORDER)]).reshape(
            2, RC, OWN
        )

    @pl.when(last[3])
    def _():
        for c in range(CHUNKS):
            backs[c, 3].wait_send()
        for r in (2, 1, 0):
            for c in range(CHUNKS):
                unless(last[1] if r == 1 else None, backs[c, r].start)

    @pl.when(takes)
    def _():
        corner.wait_recv()
        for c in range(CHUNKS):
            real = lend[c, 3, 0]
            imag = lend[c, 3, 1]
            mine = jnp.concatenate(
                [
                    jnp.concatenate([real, -imag], axis=1),
                    jnp.concatenate([imag, real], axis=1),
                ],
                axis=0,
            )
            extra = product(mine, wedge[...]).reshape(2, RC, BLK)
            for b in range(OWN // BLK):
                local[c, :, :, pl.ds(b * BLK, BLK)] += extra * weight[3][b]

    for c in range(CHUNKS):
        for r in SEND_ORDER:
            backs[c, r].wait_recv()
        for b in range(OWN // BLK):
            total = local[c, :, :, pl.ds(b * BLK, BLK)]
            for r in range(ROUNDS):
                total += arrived[c, r].astype(jnp.float32) * weight[r][b]
            out[:, pl.ds(c * RC, RC), pl.ds(b * BLK, BLK)] = total.astype(jnp.bfloat16)
    @pl.when(hub)
    def _():
        for c in range(CHUNKS):
            legs[c][1].wait_send()

    @pl.when(gives)
    def _():
        corner.wait_send()

    for c in range(CHUNKS):
        for r in range(ROUNDS):
            lends[c, r].wait_send()
            if r == 3:
                unless(last[3], backs[c, r].wait_send)
            else:
                backs[c, r].wait_send()


def solution(mesh):
    count = mesh.shape["groups"]

    def step(currents, inverse, send_blocks, send_flags):
        pieces = (CHUNKS, ROUNDS, 2, RC, BLK)
        return pl.pallas_call(
            functools.partial(kernel, count),
            out_shape=pltpu.VMEM(currents.shape, jnp.bfloat16),
            in_specs=[
                pl.BlockSpec(memory_space=pltpu.SMEM),
                pl.BlockSpec(memory_space=pltpu.SMEM),
                pl.BlockSpec(memory_space=pl.ANY),
                pl.BlockSpec(memory_space=pl.ANY),
            ],
            out_specs=pl.BlockSpec(memory_space=pltpu.VMEM),
            scratch_shapes=[
                pltpu.VMEM((2, RHS, OWN), jnp.bfloat16),
                pltpu.VMEM((ORDER, 2 * ORDER), jnp.bfloat16),
                pltpu.VMEM((CHUNKS, 2, RC, ORDER), jnp.bfloat16),
                pltpu.VMEM((CHUNKS, 2, RC, ORDER), jnp.bfloat16),
                pltpu.VMEM((CHUNKS, 2, RC, ORDER), jnp.float32),
                pltpu.VMEM(pieces, jnp.bfloat16),
                pltpu.VMEM(pieces, jnp.bfloat16),
                pltpu.VMEM(pieces, jnp.bfloat16),
                pltpu.VMEM(pieces, jnp.bfloat16),
                pltpu.SemaphoreType.DMA((5,)),
                pltpu.SemaphoreType.DMA((CHUNKS, ROUNDS)),
                pltpu.SemaphoreType.DMA((CHUNKS, ROUNDS)),
                pltpu.SemaphoreType.DMA((CHUNKS, ROUNDS)),
                pltpu.SemaphoreType.DMA((CHUNKS, ROUNDS)),
                pltpu.SemaphoreType.REGULAR((ROUNDS,)),
                pltpu.VMEM((CHUNKS, 2, RC, BLK), jnp.bfloat16),
                pltpu.SemaphoreType.DMA((CHUNKS,)),
                pltpu.SemaphoreType.DMA((CHUNKS,)),
                pltpu.VMEM((BLK, 2 * BLK), jnp.bfloat16),
                pltpu.VMEM((BLK, 2 * BLK), jnp.bfloat16),
                pltpu.SemaphoreType.DMA,
                pltpu.SemaphoreType.DMA,
            ],
            compiler_params=pltpu.CompilerParams(
                collective_id=1,
                has_side_effects=True,
                vmem_limit_bytes=60 * 1024 * 1024,
            ),
            cost_estimate=pl.CostEstimate(
                flops=8 * RHS * ORDER * ORDER,
                bytes_accessed=4 * ORDER * ORDER + 8 * RHS * OWN,
                transcendentals=0,
            ),
        )(send_blocks, send_flags, currents, inverse)

    in_specs = (
        P(None, None, "groups"),
        P("groups", None, None, None),
        P("groups", None),
        P("groups", None),
    )
    return jax.shard_map(
        step, mesh=mesh, in_specs=in_specs, out_specs=P(None, None, "groups"), check_vma=False
    )
```

```python
import functools

import jax
import jax.numpy as jnp
from jax import lax
from jax.experimental import pallas as pl
from jax.experimental.pallas import tpu as pltpu
from jax.sharding import PartitionSpec as P

MESH = pl.DeviceIdType.MESH
BLK = 128
COLS = 8
OWN = 512
ORDER = 1024
RHS = 192
ROUNDS = 4
PLANE = 128
CHUNKS = 2
RC = RHS // CHUNKS
SEND_ORDER = (3, 2, 1, 0)


def partners(me, count):
    column_odd = lax.rem(me, 2)
    line_odd = lax.rem(me // COLS, 2)
    steps = (
        1 - 2 * column_odd,
        2 * column_odd - 1,
        COLS * (1 - 2 * line_odd),
        COLS * (2 * line_odd - 1),
    )
    return [lax.rem(me + step + count, count) for step in steps]


def ends(me):
    line = lax.rem(me // COLS, PLANE // COLS)
    column = lax.rem(me, PLANE)
    first = (None, column == 0, None, line == 0)
    last = (None, column == PLANE - 1, None, line == PLANE // COLS - 1)
    return first, last, line == 1


def kernel(
    count,
    blk_hbm,
    flg_hbm,
    cur_hbm,
    inv_hbm,
    out,
    cur,
    mat,
    own,
    slot,
    local,
    lend,
    lent,
    back,
    arrived,
    load_sem,
    lend_send,
    lend_recv,
    back_send,
    back_recv,
    ready,
    blk_ref,
    flg_ref,
    relay,
    relay_send,
    relay_recv,
    edge,
    wedge,
    wedge_send,
    wedge_recv,
):
    me = lax.axis_index("groups")
    partner = partners(me, count)

    barrier = pltpu.get_barrier_semaphore()
    first, last, hub = ends(me)
    before = lax.rem(me + count - 2 * COLS, count)
    after = lax.rem(me + 2 * COLS, count)

    def greet(r):
        pl.semaphore_signal(barrier, inc=1, device_id=(partner[r],), device_id_type=MESH)

    def unless(condition, do):
        if condition is None:
            do()
        else:
            pl.when(jnp.logical_not(condition))(do)

    for r in SEND_ORDER:
        unless(last[r], functools.partial(greet, r))

    @pl.when(hub)
    def _():
        pl.semaphore_signal(barrier, inc=1, device_id=(before,), device_id_type=MESH)

    load_cur = pltpu.make_async_copy(cur_hbm, cur, load_sem.at[0])
    load_cur.start()
    load_small = [
        pltpu.make_async_copy(blk_hbm, blk_ref, load_sem.at[5]),
        pltpu.make_async_copy(flg_hbm, flg_ref, load_sem.at[6]),
    ]
    for copy in load_small:
        copy.start()
    load_mat = []
    for half in range(2):
        for part in range(2):
            load_mat.append(
                pltpu.make_async_copy(
                    inv_hbm.at[0, part, :, pl.ds(half * OWN, OWN)],
                    mat.at[:, pl.ds(half * ORDER + part * OWN, OWN)],
                    load_sem.at[1 + 2 * half + part],
                )
            )
            load_mat[-1].start()

    for copy in load_small:
        copy.wait()
    weight = [
        [
            jnp.where(blk_ref[0, r] == b, flg_ref[0, r], 0).astype(jnp.float32)
            for b in range(OWN // BLK)
        ]
        for r in range(ROUNDS)
    ]
    load_cur.wait()
    for r in range(ROUNDS):
        for c in range(CHUNKS):
            piece = jnp.zeros((2, RC, BLK), jnp.bfloat16)
            for b in range(OWN // BLK):
                block = cur[:, pl.ds(c * RC, RC), pl.ds(b * BLK, BLK)]
                piece += block * weight[r][b].astype(jnp.bfloat16)
            lend[c, r] = piece

    greeted = ROUNDS
    for r in (1, 3):
        greeted = greeted - first[r].astype(jnp.int32)
    pl.semaphore_wait(barrier, greeted + last[3].astype(jnp.int32))
    for r in (3, 1):

        @pl.when(last[r])
        def _():
            pl.semaphore_signal(
                ready.at[r], inc=1, device_id=(partner[r],), device_id_type=MESH
            )

    def remote(src, dst, send, recv, c, r):
        return pltpu.make_async_remote_copy(
            src_ref=src.at[c, r],
            dst_ref=dst.at[c, r],
            send_sem=send.at[c, r],
            recv_sem=recv.at[c, r],
            device_id=(partner[r],),
            device_id_type=MESH,
        )

    gives = last[3]
    takes = first[3]
    lends = {}
    for c in range(CHUNKS):
        for r in range(ROUNDS):
            lends[c, r] = remote(lend, lent, lend_send, lend_recv, c, r)
    legs = []
    for c in range(CHUNKS):
        legs.append(
            (
                pltpu.make_async_remote_copy(
                    src_ref=lend.at[c, 3],
                    dst_ref=relay.at[c],
                    send_sem=lend_send.at[c, 3],
                    recv_sem=relay_recv.at[c],
                    device_id=(after,),
                    device_id_type=MESH,
                ),
                pltpu.make_async_remote_copy(
                    src_ref=relay.at[c],
                    dst_ref=lent.at[c, 3],
                    send_sem=relay_send.at[c],
                    recv_sem=lend_recv.at[c, 3],
                    device_id=(partner[2],),
                    device_id_type=MESH,
                ),
            )
        )
    for c in range(CHUNKS):
        pl.when(last[3])(legs[c][0].start)
    plane_end = lax.rem(me // COLS, PLANE // COLS) == PLANE // COLS - 2
    for c in range(CHUNKS):
        for r in SEND_ORDER:
            if r == 3:
                pl.when(jnp.logical_not(first[3] | last[3] | plane_end))(lends[c, r].start)
            else:
                unless(first[r], lends[c, r].start)
    for c in range(CHUNKS):
        pl.when(plane_end)(lends[c, 3].start)

    for c in range(CHUNKS):
        real = cur[0, pl.ds(c * RC, RC), :]
        imag = cur[1, pl.ds(c * RC, RC), :]
        own[c, 0, :, pl.ds(0, OWN)] = real
        own[c, 0, :, pl.ds(OWN, OWN)] = -imag
        own[c, 1, :, pl.ds(0, OWN)] = imag
        own[c, 1, :, pl.ds(OWN, OWN)] = real

    def product(rows, matrix):
        return lax.dot_general(
            rows, matrix, (((1,), (1,)), ((), ())), preferred_element_type=jnp.float32
        )

    load_mat[0].wait()
    load_mat[1].wait()
    own_rows = own[...].reshape(2 * RHS, ORDER)
    for half in (1, 0):
        rows = pl.ds(half * OWN, OWN)
        local[:, :, :, rows] = product(own_rows, mat[rows, pl.ds(0, ORDER)]).reshape(
            CHUNKS, 2, RC, OWN
        )
    load_mat[2].wait()
    load_mat[3].wait()
    @pl.when(hub)
    def _():
        for c in range(CHUNKS):
            legs[c][0].wait_recv()
            legs[c][1].start()

    for r in (1, 3):

        @pl.when(first[r])
        def _():
            pl.semaphore_wait(ready.at[r], 1)
            for c in range(CHUNKS):
                lends[c, r].start()

    corner = pltpu.make_async_remote_copy(
        src_ref=edge,
        dst_ref=wedge,
        send_sem=wedge_send,
        recv_sem=wedge_recv,
        device_id=(partner[3],),
        device_id_type=MESH,
    )

    def fill(c, r):
        lends[c, r].wait_recv()
        real = lent[c, r, 0]
        imag = lent[c, r, 1]
        slot[c, 0, :, pl.ds(r * BLK, BLK)] = real
        slot[c, 0, :, pl.ds(OWN + r * BLK, BLK)] = -imag
        slot[c, 1, :, pl.ds(r * BLK, BLK)] = imag
        slot[c, 1, :, pl.ds(OWN + r * BLK, BLK)] = real

    backs = {}
    for c in range(CHUNKS):
        for r in range(ROUNDS):
            backs[c, r] = remote(back, arrived, back_send, back_recv, c, r)

    @pl.when(gives)
    def _():
        tail = pl.ds(ORDER - BLK, BLK)
        for part in range(2):
            edge[:, pl.ds(part * BLK, BLK)] = mat[tail, pl.ds(ORDER + (1 + part) * OWN - BLK, BLK)]
        corner.start()
        for c in range(CHUNKS):
            for r in (0, 1, 2):
                fill(c, r)
            part = local[c, :, :, tail].reshape(2 * RC, BLK)
            for half in range(2):
                part += product(
                    slot[c, :, :, pl.ds(half * OWN, OWN - BLK)].reshape(2 * RC, OWN - BLK),
                    mat[tail, pl.ds(ORDER + half * OWN, OWN - BLK)],
                )
            back[c, 3] = part.reshape(2, RC, BLK).astype(jnp.bfloat16)
            backs[c, 3].start()

    for c in range(CHUNKS):

        @pl.when(jnp.logical_not(gives))
        def _():
            for r in (0, 1, 2):
                fill(c, r)

        fill(c, 3)
        slot_rows = slot[c].reshape(2 * RC, ORDER)
        far = pl.ds(OWN, OWN)
        returned = local[c, :, :, far] + product(
            slot_rows, mat[far, pl.ds(ORDER, ORDER)]
        ).reshape(2, RC, OWN)
        for r in (2, 1, 0, 3):
            piece = returned[:, :, r * BLK : (r + 1) * BLK].astype(jnp.bfloat16)
            if r == 3:

                @pl.when(jnp.logical_not(gives))
                def _():
                    back[c, r] = piece
                    backs[c, r].start()

            else:
                back[c, r] = piece
                if r == 1:
                    pl.when(last[1] | jnp.logical_not(last[3]))(backs[c, r].start)
                else:
                    unless(last[3], backs[c, r].start)
        near = pl.ds(0, OWN)
        local[c, :, :, near] += product(slot_rows, mat[near, pl.ds(ORDER, ORDER)]).reshape(
            2, RC, OWN
        )

    @pl.when(last[3])
    def _():
        for c in range(CHUNKS):
            backs[c, 3].wait_send()
        for r in (2, 1, 0):
            for c in range(CHUNKS):
                unless(last[1] if r == 1 else None, backs[c, r].start)

    @pl.when(takes)
    def _():
        corner.wait_recv()
        for c in range(CHUNKS):
            real = lend[c, 3, 0]
            imag = lend[c, 3, 1]
            mine = jnp.concatenate(
                [
                    jnp.concatenate([real, -imag], axis=1),
                    jnp.concatenate([imag, real], axis=1),
                ],
                axis=0,
            )
            extra = product(mine, wedge[...]).reshape(2, RC, BLK)
            for b in range(OWN // BLK):
                local[c, :, :, pl.ds(b * BLK, BLK)] += extra * weight[3][b]

    for c in range(CHUNKS):
        for r in SEND_ORDER:
            backs[c, r].wait_recv()
        for b in range(OWN // BLK):
            total = local[c, :, :, pl.ds(b * BLK, BLK)]
            for r in range(ROUNDS):
                total += arrived[c, r].astype(jnp.float32) * weight[r][b]
            out[:, pl.ds(c * RC, RC), pl.ds(b * BLK, BLK)] = total.astype(jnp.bfloat16)
    @pl.when(hub)
    def _():
        for c in range(CHUNKS):
            legs[c][1].wait_send()

    @pl.when(gives)
    def _():
        corner.wait_send()

    for c in range(CHUNKS):
        for r in range(ROUNDS):
            lends[c, r].wait_send()
            if r == 3:
                unless(last[3], backs[c, r].wait_send)
            else:
                backs[c, r].wait_send()


def solution(mesh):
    count = mesh.shape["groups"]

    def step(currents, inverse, send_blocks, send_flags):
        pieces = (CHUNKS, ROUNDS, 2, RC, BLK)
        return pl.pallas_call(
            functools.partial(kernel, count),
            out_shape=pltpu.VMEM(currents.shape, jnp.bfloat16),
            in_specs=[
                pl.BlockSpec(memory_space=pl.ANY),
                pl.BlockSpec(memory_space=pl.ANY),
                pl.BlockSpec(memory_space=pl.ANY),
                pl.BlockSpec(memory_space=pl.ANY),
            ],
            out_specs=pl.BlockSpec(memory_space=pltpu.VMEM),
            scratch_shapes=[
                pltpu.VMEM((2, RHS, OWN), jnp.bfloat16),
                pltpu.VMEM((ORDER, 2 * ORDER), jnp.bfloat16),
                pltpu.VMEM((CHUNKS, 2, RC, ORDER), jnp.bfloat16),
                pltpu.VMEM((CHUNKS, 2, RC, ORDER), jnp.bfloat16),
                pltpu.VMEM((CHUNKS, 2, RC, ORDER), jnp.float32),
                pltpu.VMEM(pieces, jnp.bfloat16),
                pltpu.VMEM(pieces, jnp.bfloat16),
                pltpu.VMEM(pieces, jnp.bfloat16),
                pltpu.VMEM(pieces, jnp.bfloat16),
                pltpu.SemaphoreType.DMA((7,)),
                pltpu.SemaphoreType.DMA((CHUNKS, ROUNDS)),
                pltpu.SemaphoreType.DMA((CHUNKS, ROUNDS)),
                pltpu.SemaphoreType.DMA((CHUNKS, ROUNDS)),
                pltpu.SemaphoreType.DMA((CHUNKS, ROUNDS)),
                pltpu.SemaphoreType.REGULAR((ROUNDS,)),
                pltpu.SMEM((1, ROUNDS), jnp.int32),
                pltpu.SMEM((1, ROUNDS), jnp.int32),
                pltpu.VMEM((CHUNKS, 2, RC, BLK), jnp.bfloat16),
                pltpu.SemaphoreType.DMA((CHUNKS,)),
                pltpu.SemaphoreType.DMA((CHUNKS,)),
                pltpu.VMEM((BLK, 2 * BLK), jnp.bfloat16),
                pltpu.VMEM((BLK, 2 * BLK), jnp.bfloat16),
                pltpu.SemaphoreType.DMA,
                pltpu.SemaphoreType.DMA,
            ],
            compiler_params=pltpu.CompilerParams(
                collective_id=1,
                has_side_effects=True,
                vmem_limit_bytes=60 * 1024 * 1024,
            ),
            cost_estimate=pl.CostEstimate(
                flops=8 * RHS * ORDER * ORDER,
                bytes_accessed=4 * ORDER * ORDER + 8 * RHS * OWN,
                transcendentals=0,
            ),
        )(send_blocks, send_flags, currents, inverse)

    in_specs = (
        P(None, None, "groups"),
        P("groups", None, None, None),
        P("groups", None),
        P("groups", None),
    )
    return jax.shard_map(
        step, mesh=mesh, in_specs=in_specs, out_specs=P(None, None, "groups"), check_vma=False
    )
```

```python
import functools

import jax
import jax.numpy as jnp
from jax import lax
from jax.experimental import pallas as pl
from jax.experimental.pallas import tpu as pltpu
from jax.sharding import PartitionSpec as P

MESH = pl.DeviceIdType.MESH
BLK = 128
COLS = 8
OWN = 512
ORDER = 1024
RHS = 192
ROUNDS = 4
PLANE = 128
CHUNKS = 2
RC = RHS // CHUNKS
SEND_ORDER = (3, 2, 1, 0)


def partners(me, count):
    column_odd = lax.rem(me, 2)
    line_odd = lax.rem(me // COLS, 2)
    steps = (
        1 - 2 * column_odd,
        2 * column_odd - 1,
        COLS * (1 - 2 * line_odd),
        COLS * (2 * line_odd - 1),
    )
    return [lax.rem(me + step + count, count) for step in steps]


def ends(me):
    line = lax.rem(me // COLS, PLANE // COLS)
    column = lax.rem(me, PLANE)
    first = (None, column == 0, None, line == 0)
    last = (None, column == PLANE - 1, None, line == PLANE // COLS - 1)
    return first, last, line == 1


def kernel(
    count,
    blk_hbm,
    flg_hbm,
    cur_hbm,
    inv_hbm,
    out,
    cur,
    mat,
    own,
    slot,
    local,
    lend,
    lent,
    back,
    arrived,
    load_sem,
    lend_send,
    lend_recv,
    back_send,
    back_recv,
    ready,
    blk_ref,
    flg_ref,
    relay,
    relay_send,
    relay_recv,
    edge,
    wedge,
    wedge_send,
    wedge_recv,
):
    me = lax.axis_index("groups")
    partner = partners(me, count)

    barrier = pltpu.get_barrier_semaphore()
    first, last, hub = ends(me)
    before = lax.rem(me + count - 2 * COLS, count)
    after = lax.rem(me + 2 * COLS, count)

    def greet(r):
        pl.semaphore_signal(barrier, inc=1, device_id=(partner[r],), device_id_type=MESH)

    def unless(condition, do):
        if condition is None:
            do()
        else:
            pl.when(jnp.logical_not(condition))(do)

    for r in SEND_ORDER:
        unless(last[r], functools.partial(greet, r))

    @pl.when(hub)
    def _():
        pl.semaphore_signal(barrier, inc=1, device_id=(before,), device_id_type=MESH)

    load_cur = pltpu.make_async_copy(cur_hbm, cur, load_sem.at[0])
    load_cur.start()
    load_small = [
        pltpu.make_async_copy(blk_hbm, blk_ref, load_sem.at[5]),
        pltpu.make_async_copy(flg_hbm, flg_ref, load_sem.at[6]),
    ]
    for copy in load_small:
        copy.start()
    load_mat = []
    for half in range(2):
        for part in range(2):
            load_mat.append(
                pltpu.make_async_copy(
                    inv_hbm.at[0, part, :, pl.ds(half * OWN, OWN)],
                    mat.at[:, pl.ds(half * ORDER + part * OWN, OWN)],
                    load_sem.at[1 + 2 * half + part],
                )
            )
            load_mat[-1].start()

    for copy in load_small:
        copy.wait()
    weight = [
        [
            jnp.where(blk_ref[0, r] == b, flg_ref[0, r], 0).astype(jnp.float32)
            for b in range(OWN // BLK)
        ]
        for r in range(ROUNDS)
    ]
    load_cur.wait()
    for r in range(ROUNDS):
        for c in range(CHUNKS):
            piece = jnp.zeros((2, RC, BLK), jnp.bfloat16)
            for b in range(OWN // BLK):
                block = cur[:, pl.ds(c * RC, RC), pl.ds(b * BLK, BLK)]
                piece += block * weight[r][b].astype(jnp.bfloat16)
            lend[c, r] = piece

    greeted = ROUNDS
    for r in (1, 3):
        greeted = greeted - first[r].astype(jnp.int32)
    pl.semaphore_wait(barrier, greeted + last[3].astype(jnp.int32))
    for r in (3, 1):

        @pl.when(last[r])
        def _():
            pl.semaphore_signal(
                ready.at[r], inc=1, device_id=(partner[r],), device_id_type=MESH
            )

    def remote(src, dst, send, recv, c, r):
        return pltpu.make_async_remote_copy(
            src_ref=src.at[c, r],
            dst_ref=dst.at[c, r],
            send_sem=send.at[c, r],
            recv_sem=recv.at[c, r],
            device_id=(partner[r],),
            device_id_type=MESH,
        )

    gives = last[3]
    takes = first[3]
    lends = {}
    for c in range(CHUNKS):
        for r in range(ROUNDS):
            lends[c, r] = remote(lend, lent, lend_send, lend_recv, c, r)
    legs = []
    for c in range(CHUNKS):
        legs.append(
            (
                pltpu.make_async_remote_copy(
                    src_ref=lend.at[c, 3],
                    dst_ref=relay.at[c],
                    send_sem=lend_send.at[c, 3],
                    recv_sem=relay_recv.at[c],
                    device_id=(after,),
                    device_id_type=MESH,
                ),
                pltpu.make_async_remote_copy(
                    src_ref=relay.at[c],
                    dst_ref=lent.at[c, 3],
                    send_sem=relay_send.at[c],
                    recv_sem=lend_recv.at[c, 3],
                    device_id=(partner[2],),
                    device_id_type=MESH,
                ),
            )
        )
    for c in range(CHUNKS):
        pl.when(last[3])(legs[c][0].start)
    plane_end = lax.rem(me // COLS, PLANE // COLS) == PLANE // COLS - 2
    for c in range(CHUNKS):
        for r in SEND_ORDER:
            if r == 3:
                pl.when(jnp.logical_not(first[3] | last[3] | plane_end))(lends[c, r].start)
            else:
                unless(first[r], lends[c, r].start)
    for c in range(CHUNKS):
        pl.when(plane_end)(lends[c, 3].start)

    for c in range(CHUNKS):
        real = cur[0, pl.ds(c * RC, RC), :]
        imag = cur[1, pl.ds(c * RC, RC), :]
        own[c, 0, :, pl.ds(0, OWN)] = real
        own[c, 0, :, pl.ds(OWN, OWN)] = -imag
        own[c, 1, :, pl.ds(0, OWN)] = imag
        own[c, 1, :, pl.ds(OWN, OWN)] = real

    def product(rows, matrix):
        return lax.dot_general(
            rows, matrix, (((1,), (1,)), ((), ())), preferred_element_type=jnp.float32
        )

    load_mat[0].wait()
    load_mat[1].wait()
    own_rows = own[...].reshape(2 * RHS, ORDER)
    for half in (1, 0):
        rows = pl.ds(half * OWN, OWN)
        local[:, :, :, rows] = product(own_rows, mat[rows, pl.ds(0, ORDER)]).reshape(
            CHUNKS, 2, RC, OWN
        )
    load_mat[2].wait()
    load_mat[3].wait()
    @pl.when(hub)
    def _():
        for c in range(CHUNKS):
            legs[c][0].wait_recv()
            legs[c][1].start()

    for r in (1, 3):

        @pl.when(first[r])
        def _():
            pl.semaphore_wait(ready.at[r], 1)
            for c in range(CHUNKS):
                lends[c, r].start()

    corner = pltpu.make_async_remote_copy(
        src_ref=edge,
        dst_ref=wedge,
        send_sem=wedge_send,
        recv_sem=wedge_recv,
        device_id=(partner[3],),
        device_id_type=MESH,
    )

    def fill(c, r):
        lends[c, r].wait_recv()
        real = lent[c, r, 0]
        imag = lent[c, r, 1]
        slot[c, 0, :, pl.ds(r * BLK, BLK)] = real
        slot[c, 0, :, pl.ds(OWN + r * BLK, BLK)] = -imag
        slot[c, 1, :, pl.ds(r * BLK, BLK)] = imag
        slot[c, 1, :, pl.ds(OWN + r * BLK, BLK)] = real

    backs = {}
    for c in range(CHUNKS):
        for r in range(ROUNDS):
            backs[c, r] = remote(back, arrived, back_send, back_recv, c, r)

    @pl.when(gives)
    def _():
        tail = pl.ds(ORDER - BLK, BLK)
        for part in range(2):
            edge[:, pl.ds(part * BLK, BLK)] = mat[tail, pl.ds(ORDER + (1 + part) * OWN - BLK, BLK)]
        corner.start()
        for c in range(CHUNKS):
            for r in (0, 1, 2):
                fill(c, r)
            part = local[c, :, :, tail].reshape(2 * RC, BLK)
            for half in range(2):
                part += product(
                    slot[c, :, :, pl.ds(half * OWN, OWN - BLK)].reshape(2 * RC, OWN - BLK),
                    mat[tail, pl.ds(ORDER + half * OWN, OWN - BLK)],
                )
            back[c, 3] = part.reshape(2, RC, BLK).astype(jnp.bfloat16)
            backs[c, 3].start()

    for c in range(CHUNKS):

        @pl.when(jnp.logical_not(gives))
        def _():
            for r in (0, 1, 2):
                fill(c, r)

        fill(c, 3)
        slot_rows = slot[c].reshape(2 * RC, ORDER)
        far = pl.ds(OWN, OWN)
        returned = local[c, :, :, far] + product(
            slot_rows, mat[far, pl.ds(ORDER, ORDER)]
        ).reshape(2, RC, OWN)
        for r in (2, 1, 0, 3):
            piece = returned[:, :, r * BLK : (r + 1) * BLK].astype(jnp.bfloat16)
            if r == 3:

                @pl.when(jnp.logical_not(gives))
                def _():
                    back[c, r] = piece
                    backs[c, r].start()

            else:
                back[c, r] = piece
                if r == 1:
                    pl.when(last[1] | jnp.logical_not(last[3]))(backs[c, r].start)
                else:
                    unless(last[3], backs[c, r].start)

    @pl.when(last[3])
    def _():
        for c in range(CHUNKS):
            backs[c, 3].wait_send()
        for r in (2, 1, 0):
            for c in range(CHUNKS):
                unless(last[1] if r == 1 else None, backs[c, r].start)

    near = pl.ds(0, OWN)
    for c in range(CHUNKS):
        local[c, :, :, near] += product(
            slot[c].reshape(2 * RC, ORDER), mat[near, pl.ds(ORDER, ORDER)]
        ).reshape(2, RC, OWN)

    @pl.when(takes)
    def _():
        corner.wait_recv()
        for c in range(CHUNKS):
            real = lend[c, 3, 0]
            imag = lend[c, 3, 1]
            mine = jnp.concatenate(
                [
                    jnp.concatenate([real, -imag], axis=1),
                    jnp.concatenate([imag, real], axis=1),
                ],
                axis=0,
            )
            extra = product(mine, wedge[...]).reshape(2, RC, BLK)
            for b in range(OWN // BLK):
                local[c, :, :, pl.ds(b * BLK, BLK)] += extra * weight[3][b]

    for c in range(CHUNKS):
        for r in SEND_ORDER:
            backs[c, r].wait_recv()
        for b in range(OWN // BLK):
            total = local[c, :, :, pl.ds(b * BLK, BLK)]
            for r in range(ROUNDS):
                total += arrived[c, r].astype(jnp.float32) * weight[r][b]
            out[:, pl.ds(c * RC, RC), pl.ds(b * BLK, BLK)] = total.astype(jnp.bfloat16)
    @pl.when(hub)
    def _():
        for c in range(CHUNKS):
            legs[c][1].wait_send()

    @pl.when(gives)
    def _():
        corner.wait_send()

    for c in range(CHUNKS):
        for r in range(ROUNDS):
            lends[c, r].wait_send()
            if r == 3:
                unless(last[3], backs[c, r].wait_send)
            else:
                backs[c, r].wait_send()


def solution(mesh):
    count = mesh.shape["groups"]

    def step(currents, inverse, send_blocks, send_flags):
        pieces = (CHUNKS, ROUNDS, 2, RC, BLK)
        return pl.pallas_call(
            functools.partial(kernel, count),
            out_shape=pltpu.VMEM(currents.shape, jnp.bfloat16),
            in_specs=[
                pl.BlockSpec(memory_space=pl.ANY),
                pl.BlockSpec(memory_space=pl.ANY),
                pl.BlockSpec(memory_space=pl.ANY),
                pl.BlockSpec(memory_space=pl.ANY),
            ],
            out_specs=pl.BlockSpec(memory_space=pltpu.VMEM),
            scratch_shapes=[
                pltpu.VMEM((2, RHS, OWN), jnp.bfloat16),
                pltpu.VMEM((ORDER, 2 * ORDER), jnp.bfloat16),
                pltpu.VMEM((CHUNKS, 2, RC, ORDER), jnp.bfloat16),
                pltpu.VMEM((CHUNKS, 2, RC, ORDER), jnp.bfloat16),
                pltpu.VMEM((CHUNKS, 2, RC, ORDER), jnp.float32),
                pltpu.VMEM(pieces, jnp.bfloat16),
                pltpu.VMEM(pieces, jnp.bfloat16),
                pltpu.VMEM(pieces, jnp.bfloat16),
                pltpu.VMEM(pieces, jnp.bfloat16),
                pltpu.SemaphoreType.DMA((7,)),
                pltpu.SemaphoreType.DMA((CHUNKS, ROUNDS)),
                pltpu.SemaphoreType.DMA((CHUNKS, ROUNDS)),
                pltpu.SemaphoreType.DMA((CHUNKS, ROUNDS)),
                pltpu.SemaphoreType.DMA((CHUNKS, ROUNDS)),
                pltpu.SemaphoreType.REGULAR((ROUNDS,)),
                pltpu.SMEM((1, ROUNDS), jnp.int32),
                pltpu.SMEM((1, ROUNDS), jnp.int32),
                pltpu.VMEM((CHUNKS, 2, RC, BLK), jnp.bfloat16),
                pltpu.SemaphoreType.DMA((CHUNKS,)),
                pltpu.SemaphoreType.DMA((CHUNKS,)),
                pltpu.VMEM((BLK, 2 * BLK), jnp.bfloat16),
                pltpu.VMEM((BLK, 2 * BLK), jnp.bfloat16),
                pltpu.SemaphoreType.DMA,
                pltpu.SemaphoreType.DMA,
            ],
            compiler_params=pltpu.CompilerParams(
                collective_id=1,
                has_side_effects=True,
                vmem_limit_bytes=60 * 1024 * 1024,
            ),
            cost_estimate=pl.CostEstimate(
                flops=8 * RHS * ORDER * ORDER,
                bytes_accessed=4 * ORDER * ORDER + 8 * RHS * OWN,
                transcendentals=0,
            ),
        )(send_blocks, send_flags, currents, inverse)

    in_specs = (
        P(None, None, "groups"),
        P("groups", None, None, None),
        P("groups", None),
        P("groups", None),
    )
    return jax.shard_map(
        step, mesh=mesh, in_specs=in_specs, out_specs=P(None, None, "groups"), check_vma=False
    )
```

```python
import functools

import jax
import jax.numpy as jnp
from jax import lax
from jax.experimental import pallas as pl
from jax.experimental.pallas import tpu as pltpu
from jax.sharding import PartitionSpec as P

MESH = pl.DeviceIdType.MESH
BLK = 128
COLS = 8
OWN = 512
ORDER = 1024
RHS = 192
ROUNDS = 4
PLANE = 128
CHUNKS = 2
RC = RHS // CHUNKS
SEND_ORDER = (3, 2, 1, 0)


def partners(me, count):
    column_odd = lax.rem(me, 2)
    line_odd = lax.rem(me // COLS, 2)
    steps = (
        1 - 2 * column_odd,
        2 * column_odd - 1,
        COLS * (1 - 2 * line_odd),
        COLS * (2 * line_odd - 1),
    )
    return [lax.rem(me + step + count, count) for step in steps]


def ends(me):
    line = lax.rem(me // COLS, PLANE // COLS)
    column = lax.rem(me, PLANE)
    first = (None, column == 0, None, line == 0)
    last = (None, column == PLANE - 1, None, line == PLANE // COLS - 1)
    return first, last, line == 1


def kernel(
    count,
    blk_hbm,
    flg_hbm,
    cur_hbm,
    inv_hbm,
    out,
    cur,
    mat,
    own,
    slot,
    local,
    lend,
    lent,
    back,
    arrived,
    load_sem,
    lend_send,
    lend_recv,
    back_send,
    back_recv,
    ready,
    blk_ref,
    flg_ref,
    relay,
    relay_send,
    relay_recv,
    edge,
    wedge,
    wedge_send,
    wedge_recv,
):
    me = lax.axis_index("groups")
    partner = partners(me, count)

    barrier = pltpu.get_barrier_semaphore()
    first, last, hub = ends(me)
    before = lax.rem(me + count - 2 * COLS, count)
    after = lax.rem(me + 2 * COLS, count)

    def greet(r):
        pl.semaphore_signal(barrier, inc=1, device_id=(partner[r],), device_id_type=MESH)

    def unless(condition, do):
        if condition is None:
            do()
        else:
            pl.when(jnp.logical_not(condition))(do)

    for r in SEND_ORDER:
        unless(last[r], functools.partial(greet, r))

    @pl.when(hub)
    def _():
        pl.semaphore_signal(barrier, inc=1, device_id=(before,), device_id_type=MESH)

    load_cur = pltpu.make_async_copy(cur_hbm, cur, load_sem.at[0])
    load_cur.start()
    load_small = [
        pltpu.make_async_copy(blk_hbm, blk_ref, load_sem.at[5]),
        pltpu.make_async_copy(flg_hbm, flg_ref, load_sem.at[6]),
    ]
    for copy in load_small:
        copy.start()
    load_mat = []
    for half in range(2):
        for part in range(2):
            load_mat.append(
                pltpu.make_async_copy(
                    inv_hbm.at[0, part, :, pl.ds(half * OWN, OWN)],
                    mat.at[:, pl.ds(half * ORDER + part * OWN, OWN)],
                    load_sem.at[1 + 2 * half + part],
                )
            )
            load_mat[-1].start()

    for copy in load_small:
        copy.wait()
    weight = [
        [
            jnp.where(blk_ref[0, r] == b, flg_ref[0, r], 0).astype(jnp.float32)
            for b in range(OWN // BLK)
        ]
        for r in range(ROUNDS)
    ]
    load_cur.wait()
    for r in range(ROUNDS):
        for c in range(CHUNKS):
            piece = jnp.zeros((2, RC, BLK), jnp.bfloat16)
            for b in range(OWN // BLK):
                block = cur[:, pl.ds(c * RC, RC), pl.ds(b * BLK, BLK)]
                piece += block * weight[r][b].astype(jnp.bfloat16)
            lend[c, r] = piece

    greeted = ROUNDS
    for r in (1, 3):
        greeted = greeted - first[r].astype(jnp.int32)
    pl.semaphore_wait(barrier, greeted + last[3].astype(jnp.int32))
    for r in (3, 1):

        @pl.when(last[r])
        def _():
            pl.semaphore_signal(
                ready.at[r], inc=1, device_id=(partner[r],), device_id_type=MESH
            )

    def remote(src, dst, send, recv, c, r):
        return pltpu.make_async_remote_copy(
            src_ref=src.at[c, r],
            dst_ref=dst.at[c, r],
            send_sem=send.at[c, r],
            recv_sem=recv.at[c, r],
            device_id=(partner[r],),
            device_id_type=MESH,
        )

    gives = last[3]
    takes = first[3]
    lends = {}
    for c in range(CHUNKS):
        for r in range(ROUNDS):
            lends[c, r] = remote(lend, lent, lend_send, lend_recv, c, r)
    legs = []
    for c in range(CHUNKS):
        legs.append(
            (
                pltpu.make_async_remote_copy(
                    src_ref=lend.at[c, 3],
                    dst_ref=relay.at[c],
                    send_sem=lend_send.at[c, 3],
                    recv_sem=relay_recv.at[c],
                    device_id=(after,),
                    device_id_type=MESH,
                ),
                pltpu.make_async_remote_copy(
                    src_ref=relay.at[c],
                    dst_ref=lent.at[c, 3],
                    send_sem=relay_send.at[c],
                    recv_sem=lend_recv.at[c, 3],
                    device_id=(partner[2],),
                    device_id_type=MESH,
                ),
            )
        )
    for c in range(CHUNKS):
        pl.when(last[3])(legs[c][0].start)
    plane_end = lax.rem(me // COLS, PLANE // COLS) == PLANE // COLS - 2
    for c in range(CHUNKS):
        for r in SEND_ORDER:
            if r == 3:
                pl.when(jnp.logical_not(first[3] | last[3] | plane_end))(lends[c, r].start)
            else:
                unless(first[r], lends[c, r].start)
    for c in range(CHUNKS):
        pl.when(plane_end)(lends[c, 3].start)

    for c in range(CHUNKS):
        real = cur[0, pl.ds(c * RC, RC), :]
        imag = cur[1, pl.ds(c * RC, RC), :]
        own[c, 0, :, pl.ds(0, OWN)] = real
        own[c, 0, :, pl.ds(OWN, OWN)] = -imag
        own[c, 1, :, pl.ds(0, OWN)] = imag
        own[c, 1, :, pl.ds(OWN, OWN)] = real

    def product(rows, matrix):
        return lax.dot_general(
            rows, matrix, (((1,), (1,)), ((), ())), preferred_element_type=jnp.float32
        )

    load_mat[0].wait()
    load_mat[1].wait()
    own_rows = own[...].reshape(2 * RHS, ORDER)
    for half in (1, 0):
        rows = pl.ds(half * OWN, OWN)
        local[:, :, :, rows] = product(own_rows, mat[rows, pl.ds(0, ORDER)]).reshape(
            CHUNKS, 2, RC, OWN
        )
    load_mat[2].wait()
    load_mat[3].wait()
    @pl.when(hub)
    def _():
        for c in range(CHUNKS):
            legs[c][0].wait_recv()
            legs[c][1].start()

    for r in (1, 3):

        @pl.when(first[r])
        def _():
            pl.semaphore_wait(ready.at[r], 1)
            for c in range(CHUNKS):
                lends[c, r].start()

    corner = pltpu.make_async_remote_copy(
        src_ref=edge,
        dst_ref=wedge,
        send_sem=wedge_send,
        recv_sem=wedge_recv,
        device_id=(partner[3],),
        device_id_type=MESH,
    )

    def fill(c, r):
        lends[c, r].wait_recv()
        real = lent[c, r, 0]
        imag = lent[c, r, 1]
        slot[c, 0, :, pl.ds(r * BLK, BLK)] = real
        slot[c, 0, :, pl.ds(OWN + r * BLK, BLK)] = -imag
        slot[c, 1, :, pl.ds(r * BLK, BLK)] = imag
        slot[c, 1, :, pl.ds(OWN + r * BLK, BLK)] = real

    backs = {}
    for c in range(CHUNKS):
        for r in range(ROUNDS):
            backs[c, r] = remote(back, arrived, back_send, back_recv, c, r)

    @pl.when(gives)
    def _():
        tail = pl.ds(ORDER - BLK, BLK)
        for part in range(2):
            edge[:, pl.ds(part * BLK, BLK)] = mat[tail, pl.ds(ORDER + (1 + part) * OWN - BLK, BLK)]
        corner.start()
        for c in range(CHUNKS):
            for r in (0, 1, 2):
                fill(c, r)
            part = local[c, :, :, tail].reshape(2 * RC, BLK)
            for half in range(2):
                part += product(
                    slot[c, :, :, pl.ds(half * OWN, OWN - BLK)].reshape(2 * RC, OWN - BLK),
                    mat[tail, pl.ds(ORDER + half * OWN, OWN - BLK)],
                )
            back[c, 3] = part.reshape(2, RC, BLK).astype(jnp.bfloat16)
            backs[c, 3].start()

    for c in range(CHUNKS):

        @pl.when(jnp.logical_not(gives))
        def _():
            for r in (0, 1, 2):
                fill(c, r)

        fill(c, 3)
        slot_rows = slot[c].reshape(2 * RC, ORDER)
        far = pl.ds(OWN, OWN)
        returned = local[c, :, :, far] + product(
            slot_rows, mat[far, pl.ds(ORDER, ORDER)]
        ).reshape(2, RC, OWN)
        for r in (2, 1, 0, 3):
            piece = returned[:, :, r * BLK : (r + 1) * BLK].astype(jnp.bfloat16)
            if r == 3:

                @pl.when(jnp.logical_not(gives))
                def _():
                    back[c, r] = piece
                    backs[c, r].start()

            else:
                back[c, r] = piece
                if r == 1:
                    pl.when(last[1] | jnp.logical_not(last[3]))(backs[c, r].start)
                else:
                    unless(last[3], backs[c, r].start)
        near = pl.ds(0, OWN)
        local[c, :, :, near] += product(slot_rows, mat[near, pl.ds(ORDER, ORDER)]).reshape(
            2, RC, OWN
        )

    @pl.when(last[3])
    def _():
        for c in range(CHUNKS):
            backs[c, 3].wait_send()
        for r in (2, 1, 0):
            for c in range(CHUNKS):
                unless(last[1] if r == 1 else None, backs[c, r].start)

    @pl.when(takes)
    def _():
        corner.wait_recv()
        for c in range(CHUNKS):
            real = lend[c, 3, 0]
            imag = lend[c, 3, 1]
            mine = jnp.concatenate(
                [
                    jnp.concatenate([real, -imag], axis=1),
                    jnp.concatenate([imag, real], axis=1),
                ],
                axis=0,
            )
            extra = product(mine, wedge[...]).reshape(2, RC, BLK)
            for b in range(OWN // BLK):
                local[c, :, :, pl.ds(b * BLK, BLK)] += extra * weight[3][b]

    for c in range(CHUNKS):
        for r in (0, 1, 2):
            backs[c, r].wait_recv()
        for b in range(OWN // BLK):
            total = local[c, :, :, pl.ds(b * BLK, BLK)]
            for r in (0, 1, 2):
                total += arrived[c, r].astype(jnp.float32) * weight[r][b]
            local[c, :, :, pl.ds(b * BLK, BLK)] = total
        backs[c, 3].wait_recv()
        for b in range(OWN // BLK):
            total = local[c, :, :, pl.ds(b * BLK, BLK)]
            total += arrived[c, 3].astype(jnp.float32) * weight[3][b]
            out[:, pl.ds(c * RC, RC), pl.ds(b * BLK, BLK)] = total.astype(jnp.bfloat16)
    @pl.when(hub)
    def _():
        for c in range(CHUNKS):
            legs[c][1].wait_send()

    @pl.when(gives)
    def _():
        corner.wait_send()

    for c in range(CHUNKS):
        for r in range(ROUNDS):
            lends[c, r].wait_send()
            if r == 3:
                unless(last[3], backs[c, r].wait_send)
            else:
                backs[c, r].wait_send()


def solution(mesh):
    count = mesh.shape["groups"]

    def step(currents, inverse, send_blocks, send_flags):
        pieces = (CHUNKS, ROUNDS, 2, RC, BLK)
        return pl.pallas_call(
            functools.partial(kernel, count),
            out_shape=pltpu.VMEM(currents.shape, jnp.bfloat16),
            in_specs=[
                pl.BlockSpec(memory_space=pl.ANY),
                pl.BlockSpec(memory_space=pl.ANY),
                pl.BlockSpec(memory_space=pl.ANY),
                pl.BlockSpec(memory_space=pl.ANY),
            ],
            out_specs=pl.BlockSpec(memory_space=pltpu.VMEM),
            scratch_shapes=[
                pltpu.VMEM((2, RHS, OWN), jnp.bfloat16),
                pltpu.VMEM((ORDER, 2 * ORDER), jnp.bfloat16),
                pltpu.VMEM((CHUNKS, 2, RC, ORDER), jnp.bfloat16),
                pltpu.VMEM((CHUNKS, 2, RC, ORDER), jnp.bfloat16),
                pltpu.VMEM((CHUNKS, 2, RC, ORDER), jnp.float32),
                pltpu.VMEM(pieces, jnp.bfloat16),
                pltpu.VMEM(pieces, jnp.bfloat16),
                pltpu.VMEM(pieces, jnp.bfloat16),
                pltpu.VMEM(pieces, jnp.bfloat16),
                pltpu.SemaphoreType.DMA((7,)),
                pltpu.SemaphoreType.DMA((CHUNKS, ROUNDS)),
                pltpu.SemaphoreType.DMA((CHUNKS, ROUNDS)),
                pltpu.SemaphoreType.DMA((CHUNKS, ROUNDS)),
                pltpu.SemaphoreType.DMA((CHUNKS, ROUNDS)),
                pltpu.SemaphoreType.REGULAR((ROUNDS,)),
                pltpu.SMEM((1, ROUNDS), jnp.int32),
                pltpu.SMEM((1, ROUNDS), jnp.int32),
                pltpu.VMEM((CHUNKS, 2, RC, BLK), jnp.bfloat16),
                pltpu.SemaphoreType.DMA((CHUNKS,)),
                pltpu.SemaphoreType.DMA((CHUNKS,)),
                pltpu.VMEM((BLK, 2 * BLK), jnp.bfloat16),
                pltpu.VMEM((BLK, 2 * BLK), jnp.bfloat16),
                pltpu.SemaphoreType.DMA,
                pltpu.SemaphoreType.DMA,
            ],
            compiler_params=pltpu.CompilerParams(
                collective_id=1,
                has_side_effects=True,
                vmem_limit_bytes=60 * 1024 * 1024,
            ),
            cost_estimate=pl.CostEstimate(
                flops=8 * RHS * ORDER * ORDER,
                bytes_accessed=4 * ORDER * ORDER + 8 * RHS * OWN,
                transcendentals=0,
            ),
        )(send_blocks, send_flags, currents, inverse)

    in_specs = (
        P(None, None, "groups"),
        P("groups", None, None, None),
        P("groups", None),
        P("groups", None),
    )
    return jax.shard_map(
        step, mesh=mesh, in_specs=in_specs, out_specs=P(None, None, "groups"), check_vma=False
    )
```
